32 devices in a mesh: seq: 8 (over y, x, core), head: 4 (over z).
Axes of the slice: x: 2, y: 2, z: 4, core: 2. Of those that a mesh axis runs over, the one named last changes fastest.
Arguments:
- queries: bfloat16 [8192, 8192], P(('seq', 'head')), may hold values from -6 to 6
- key_vectors: bfloat16 [8192, 8192], P(('seq', 'head')), may hold values from -6 to 6
- value_vectors: bfloat16 [8192, 8192], P(('seq', 'head')), may hold values from -6 to 6
- out_gain: float32 [64, 128], P('head'), may hold values from 0.1 to 1.9
Outputs:
- attended: bfloat16 [8192, 8192], P(('seq', 'head'))
The draws below stay inside these ranges and needn't reach their ends.
All inputs are finite; a program needn't handle non-finite values.
Results may differ from the reference program's by a relative error of at most 0.0049.
Values may be sent and summed in bfloat16 or wider, within the bound.
No kernel may reach another device: no remote copies, remote signals or barrier semaphores. Data moves between devices by JAX's collectives and lax.ppermute only.
A program may use at most 128 MiB of HBM per device.

```python
import jax
import jax.numpy as jnp
from jax import lax

HEADS = 64
HD = 128
BLOCK = 512
SEQLEN = 8192


def steps_of(own_key, dims, split, low, top_value):
    factor_of, own = 1.0, jax.random.fold_in(own_key, 6)
    for dim, blocks in split:
        draws = jnp.exp(jax.random.uniform(jax.random.fold_in(own, dim), (blocks,), jnp.float32, low / len(split), top_value / len(split)))
        factor_of = factor_of * jnp.repeat(draws, dims[dim] // blocks).reshape([-1 if axis == dim else 1 for axis in range(len(dims))])
    return factor_of


def gaussian(rng, extent, spread, bound, split=(), kind=jnp.bfloat16):
    drawn = spread * jax.random.normal(rng, extent, jnp.float32)
    if split:
        drawn = drawn * steps_of(rng, extent, split, -0.22, 0.18)
    return jnp.clip(drawn, -bound, bound).astype(kind)


def setup_inputs(seed: int = 0) -> dict:
    arg_keys = jax.random.split(jax.random.key(seed), 5)
    return {
        "queries": gaussian(arg_keys[0], (SEQLEN, HEADS * HD), 1.0, 6.0, ((0, 32),)),
        "key_vectors": gaussian(arg_keys[1], (SEQLEN, HEADS * HD), 1.0, 6.0, ((0, 32),)),
        "value_vectors": gaussian(arg_keys[2], (SEQLEN, HEADS * HD), 1.0, 6.0, ((0, 32),)),
        "out_gain": jnp.clip(1.0 + 0.18 * jax.random.normal(arg_keys[3], (HEADS, HD), jnp.float32), 0.1, 1.9),
    }


def reference(queries, key_vectors, value_vectors, out_gain):
    count = queries.shape[0] // BLOCK
    query_blocks = queries.reshape(count, BLOCK, HEADS, HD)
    key_blocks = key_vectors.reshape(count, BLOCK, HEADS, HD)
    value_blocks = value_vectors.reshape(count, BLOCK, HEADS, HD)
    causal = jnp.arange(BLOCK)[:, None] >= jnp.arange(BLOCK)[None, :]
    highest = lax.Precision.HIGHEST

    def one_head(index):
        query_f = lax.dynamic_index_in_dim(query_blocks, index, 2, keepdims=False).astype(jnp.float32)
        key_f = lax.dynamic_index_in_dim(key_blocks, index, 2, keepdims=False).astype(jnp.float32)
        value_f = lax.dynamic_index_in_dim(value_blocks, index, 2, keepdims=False).astype(jnp.float32)
        states = jnp.einsum('nbd,nbe->nde', key_f, value_f, precision=highest)
        carried = (jnp.cumsum(states, axis=0) - states).astype(jnp.bfloat16)
        carried = lax.optimization_barrier(carried).astype(jnp.float32)
        inter = jnp.einsum('nbd,nde->nbe', query_f, carried, precision=highest)
        scores = jnp.einsum('nbd,ncd->nbc', query_f, key_f, precision=highest)
        scores = jnp.where(causal[None], scores, jnp.float32(0.0)).astype(jnp.bfloat16)
        scores = lax.optimization_barrier(scores).astype(jnp.float32)
        intra = jnp.einsum('nbc,ncd->nbd', scores, value_f, precision=highest)
        raw = inter + intra
        gain_row = lax.dynamic_index_in_dim(out_gain, index, 0, keepdims=False)
        scale = lax.rsqrt(lax.optimization_barrier(jnp.mean(raw * raw, axis=-1, keepdims=True)) + 1e-06)
        return (raw * scale * gain_row).astype(jnp.bfloat16)
    result = lax.map(one_head, jnp.arange(HEADS, dtype=jnp.int32))
    result = jnp.transpose(result, (1, 2, 0, 3))
    return result.reshape(count * BLOCK, HEADS * HD)
```

```python
import functools

import jax
import jax.numpy as jnp
from jax import lax
from jax.experimental import pallas as pl
from jax.experimental.pallas import tpu as pltpu
from jax.sharding import PartitionSpec as P

HD = 128
CHUNKS = 4
STATE_HEADS = 4
OUT_HEADS = 4


def state_kernel(key_ref, value_ref, state_ref):
    for head in range(state_ref.shape[0]):
        columns = slice(head * HD, (head + 1) * HD)
        state = lax.dot_general(
            key_ref[:, columns],
            value_ref[:, columns],
            (((0,), (0,)), ((), ())),
            preferred_element_type=jnp.float32,
        )
        state_ref[head] = state.astype(jnp.bfloat16)


def states_of(key_vectors, value_vectors, first, count):
    tokens = key_vectors.shape[0]
    step = min(STATE_HEADS, count)
    tokens_spec = pl.BlockSpec((tokens, step * HD), lambda i: (0, first // step + i))
    return pl.pallas_call(
        state_kernel,
        grid=(count // step,),
        in_specs=[tokens_spec, tokens_spec],
        out_specs=pl.BlockSpec((step, HD, HD), lambda i: (i, 0, 0)),
        out_shape=jax.ShapeDtypeStruct((count, HD, HD), jnp.bfloat16),
        cost_estimate=pl.CostEstimate(
            flops=2 * tokens * HD * HD * count,
            bytes_accessed=2 * count * HD * (2 * tokens + HD),
            transcendentals=0,
        ),
    )(key_vectors, value_vectors)


def output_kernel(query_ref, key_ref, value_ref, carried_ref, gain_ref, out_ref):
    tokens = query_ref.shape[0]
    rows = lax.broadcasted_iota(jnp.int32, (tokens, tokens), 0)
    causal = rows >= lax.broadcasted_iota(jnp.int32, (tokens, tokens), 1)
    for head in range(carried_ref.shape[0]):
        columns = slice(head * HD, (head + 1) * HD)
        query = query_ref[:, columns]
        scores = lax.dot_general(
            query,
            key_ref[:, columns],
            (((1,), (1,)), ((), ())),
            preferred_element_type=jnp.float32,
        )
        scores = jnp.where(causal, scores, 0.0).astype(jnp.bfloat16)
        raw = jnp.dot(query, carried_ref[head], preferred_element_type=jnp.float32)
        raw += jnp.dot(scores, value_ref[:, columns], preferred_element_type=jnp.float32)
        scale = lax.rsqrt(jnp.mean(raw * raw, axis=-1, keepdims=True) + 1e-06)
        out_ref[:, columns] = (raw * scale * gain_ref[head]).astype(jnp.bfloat16)


def outputs_of(queries, key_vectors, value_vectors, carried, gain, first):
    tokens, count = queries.shape[0], carried.shape[0]
    step = min(OUT_HEADS, count)
    tokens_spec = pl.BlockSpec((tokens, step * HD), lambda i: (0, first // step + i))
    return pl.pallas_call(
        output_kernel,
        grid=(count // step,),
        in_specs=[
            tokens_spec,
            tokens_spec,
            tokens_spec,
            pl.BlockSpec((step, HD, HD), lambda i: (i, 0, 0)),
            pl.BlockSpec((step, 1, HD), lambda i: (first // step + i, 0, 0)),
        ],
        out_specs=pl.BlockSpec((tokens, step * HD), lambda i: (0, i)),
        out_shape=jax.ShapeDtypeStruct((tokens, count * HD), jnp.bfloat16),
        cost_estimate=pl.CostEstimate(
            flops=2 * tokens * HD * count * (2 * tokens + HD),
            bytes_accessed=2 * count * HD * (4 * tokens + HD),
            transcendentals=tokens * count,
        ),
    )(queries, key_vectors, value_vectors, carried, gain)


def added(*terms):
    return functools.reduce(jnp.add, [term.astype(jnp.float32) for term in terms])


def packed(total):
    return total.astype(jnp.bfloat16)


def carried_of(states):
    place, line = lax.axis_index("head"), lax.axis_size("head")
    shard, shards = lax.axis_index("seq"), lax.axis_size("seq")

    arrived = []
    for hop in range(1, line):
        sent = packed(added(arrived[-1], states)) if arrived else states
        route = [(hop - 1, hop), (line - hop, line - hop - 1)]
        arrived.append(lax.ppermute(sent, "head", route))
    carried = added(*[jnp.where(place == hop + 1, block, jnp.zeros_like(block)) for hop, block in enumerate(arrived)])
    total = added(states, *arrived)

    earlier = jnp.zeros_like(total)
    whole = total
    step = 2
    while step < shards:
        last = 2 * step == shards
        route = [(i, i ^ step) for i in range(shards) if not last or not i & step]
        block = lax.ppermute(packed(whole), "seq", route).astype(jnp.float32)
        earlier += jnp.where(shard & step != 0, block, 0.0)
        whole += block
        step *= 2

    sent = packed(earlier + jnp.where(shard & 1 == 0, total, 0.0))
    block = lax.ppermute(sent, "seq", [(i, i ^ 1) for i in range(shards)])
    return packed(carried + earlier + block.astype(jnp.float32))


def per_device(queries, key_vectors, value_vectors, out_gain):
    heads = queries.shape[1] // HD
    gain = lax.all_gather(out_gain, "head", axis=0, tiled=True).reshape(heads, 1, HD)
    count = heads // CHUNKS
    outs = []
    for first in range(0, heads, count):
        states = states_of(key_vectors, value_vectors, first, count)
        carried = carried_of(states)
        outs.append(outputs_of(queries, key_vectors, value_vectors, carried, gain, first))
    return jnp.concatenate(outs, axis=1)


def solution(mesh):
    return jax.shard_map(
        per_device,
        mesh=mesh,
        in_specs=(
            P(("seq", "head"), None),
            P(("seq", "head"), None),
            P(("seq", "head"), None),
            P("head", None),
        ),
        out_specs=P(("seq", "head"), None),
        check_vma=False,
    )
```

```python
import functools

import jax
import jax.numpy as jnp
from jax import lax
from jax.experimental import pallas as pl
from jax.experimental.pallas import tpu as pltpu
from jax.sharding import PartitionSpec as P

HD = 128
SIZES = ((16, 1),) * 4
LOCAL_STEP = 8
LOCAL_SWAP = 4
LOCAL_TIE = True
STEPS = "0 1 2 3 0 1,01 2,11 3,21 0 1 2 3 0 1 2 3 0 1 2 3 0 1 2 3 0 1 2 3"
VMEM = 24 << 20


def f32(block):
    return block.astype(jnp.float32)


def packed(total):
    return total.astype(jnp.bfloat16)


def added(*terms):
    return functools.reduce(jnp.add, [f32(term) for term in terms])


def kept(condition, block):
    return jnp.where(condition, f32(block), 0.0)


def state_kernel(side_ref, key_ref, value_ref, mine_ref, theirs_ref):
    half = mine_ref.shape[0]
    for side, state_ref in enumerate((mine_ref, theirs_ref)):
        base = (side_ref[0] ^ side) * half
        for head in range(half):
            columns = pl.ds(pl.multiple_of((base + head) * HD, HD), HD)
            state = lax.dot_general(
                key_ref[:, columns],
                value_ref[:, columns],
                (((0,), (0,)), ((), ())),
                preferred_element_type=jnp.float32,
            )
            state_ref[head] = packed(state)


def states_of(side, key_vectors, value_vectors, first, step, steps):
    tokens, half = key_vectors.shape[0], step // 2
    tokens_spec = pl.BlockSpec((tokens, step * HD), lambda i, side: (0, first // step + i))
    side_spec = pl.BlockSpec((half, HD, HD), lambda i, side: (i, 0, 0))
    half_shape = jax.ShapeDtypeStruct((steps * half, HD, HD), jnp.bfloat16)
    return pl.pallas_call(
        state_kernel,
        grid_spec=pltpu.PrefetchScalarGridSpec(
            num_scalar_prefetch=1,
            grid=(steps,),
            in_specs=[tokens_spec, tokens_spec],
            out_specs=[side_spec, side_spec],
        ),
        out_shape=[half_shape, half_shape],
        compiler_params=pltpu.CompilerParams(vmem_limit_bytes=VMEM),
        cost_estimate=pl.CostEstimate(
            flops=2 * tokens * HD * HD * step * steps,
            bytes_accessed=2 * step * steps * HD * (2 * tokens + HD),
            transcendentals=0,
        ),
    )(side, key_vectors, value_vectors)


def local_kernel(query_ref, key_ref, value_ref, local_ref):
    tokens = query_ref.shape[0]
    rows = lax.broadcasted_iota(jnp.int32, (tokens, tokens), 0)
    causal = rows >= lax.broadcasted_iota(jnp.int32, (tokens, tokens), 1)
    for head in range(query_ref.shape[1] // HD):
        columns = slice(head * HD, (head + 1) * HD)
        scores = lax.dot_general(
            query_ref[:, columns],
            key_ref[:, columns],
            (((1,), (1,)), ((), ())),
            preferred_element_type=jnp.float32,
        )
        scores = packed(jnp.where(causal, scores, 0.0))
        local_ref[:, columns] = jnp.dot(scores, value_ref[:, columns], preferred_element_type=jnp.float32)


def locals_of(queries, key_vectors, value_vectors, first, count):
    tokens, step = queries.shape[0], min(count, LOCAL_STEP)
    tokens_spec = pl.BlockSpec((tokens, step * HD), lambda i: (0, first // step + i))
    return pl.pallas_call(
        local_kernel,
        grid=(count // step,),
        in_specs=[tokens_spec] * 3,
        out_specs=pl.BlockSpec((tokens, step * HD), lambda i: (0, i)),
        out_shape=jax.ShapeDtypeStruct((tokens, count * HD), jnp.float32),
        compiler_params=pltpu.CompilerParams(vmem_limit_bytes=VMEM),
        cost_estimate=pl.CostEstimate(
            flops=4 * tokens * HD * count * tokens,
            bytes_accessed=count * HD * 10 * tokens,
            transcendentals=0,
        ),
    )(queries, key_vectors, value_vectors)


def output_kernel(side_ref, query_ref, local_ref, mine_ref, theirs_ref, gain_ref, *refs):
    out_ref = refs[-1]
    own = pl.program_id(0) == 0
    for head in range(mine_ref.shape[0]):
        columns = slice(head * HD, (head + 1) * HD)
        carried = jnp.where(own, mine_ref[head], theirs_ref[head])
        raw = jnp.dot(query_ref[:, columns], carried, preferred_element_type=jnp.float32) + local_ref[:, columns]
        scale = lax.rsqrt(jnp.mean(raw * raw, axis=-1, keepdims=True) + 1e-06)
        out_ref[:, columns] = packed(raw * scale * gain_ref[head])


def outputs_of(side, queries, local, mine, theirs, gain, first, before):
    tokens, half = queries.shape[0], mine.shape[0]
    tokens_spec = pl.BlockSpec((tokens, half * HD), lambda i, side: (0, first // half + (side[0] ^ i)))
    local_spec = pl.BlockSpec((tokens, half * HD), lambda i, side: (0, side[0] ^ i))
    side_spec = pl.BlockSpec((half, HD, HD), lambda i, side: (0, 0, 0))
    gain_spec = pl.BlockSpec((half, 1, HD), lambda i, side: (first // half + (side[0] ^ i), 0, 0))
    operands = [queries, local, mine, theirs, gain]
    in_specs = [tokens_spec, local_spec, side_spec, side_spec, gain_spec]
    aliases = {}
    if before is not None:
        operands.append(before)
        in_specs.append(pl.BlockSpec(memory_space=pl.ANY))
        aliases = {6: 0}
    return pl.pallas_call(
        output_kernel,
        grid_spec=pltpu.PrefetchScalarGridSpec(
            num_scalar_prefetch=1, grid=(2,), in_specs=in_specs, out_specs=tokens_spec
        ),
        out_shape=jax.ShapeDtypeStruct(queries.shape, jnp.bfloat16),
        input_output_aliases=aliases,
        compiler_params=pltpu.CompilerParams(vmem_limit_bytes=VMEM),
        cost_estimate=pl.CostEstimate(
            flops=4 * tokens * HD * half * HD,
            bytes_accessed=2 * half * HD * (8 * tokens + HD),
            transcendentals=2 * tokens * half,
        ),
    )(side, *operands)


def after(block, done):
    return lax.optimization_barrier((block, *done))[0] if done else block


def swapped(block, axis, step):
    return lax.ppermute(block, axis, [(i, i ^ step) for i in range(lax.axis_size(axis))])


def scan_of(mine, theirs, extra):
    half, side = mine.shape[0], lax.axis_index("head") % 2
    done = yield
    sent = theirs if extra is None else jnp.concatenate([theirs, extra])
    arrived = swapped(after(sent, done), "head", 1)
    arrived = after(arrived, (yield arrived))
    neighbour = arrived[:half]
    whole = added(mine, neighbour)
    if extra is not None:
        extra = added(extra, arrived[half:])
    earlier = jnp.zeros_like(whole)
    for axis, step in [("head", 2), ("seq", 1)]:
        index = lax.axis_index(axis)
        while step < lax.axis_size(axis):
            sent = packed(whole)
            with_extra = extra is not None and axis == "head"
            if with_extra:
                sent = jnp.concatenate([sent, packed(extra)])
            arrived = swapped(sent, axis, step)
            if (axis, step) in (("head", 2), ("seq", 1), ("seq", 2), ("seq", 4)):
                arrived = after(arrived, (yield arrived))
            earlier += kept(index & step != 0, arrived[:half])
            whole += f32(arrived[:half])
            if with_extra:
                extra = extra + f32(arrived[half:])
            step *= 2
    carried_mine = packed(earlier + kept(side == 1, neighbour))
    carried_theirs = packed(earlier + kept(side == 0, mine))
    arrived = swapped(carried_theirs, "head", 1)
    arrived = after(arrived, (yield arrived))
    yield carried_mine, arrived, extra


def parts_of(gain, heads):
    rows = jnp.zeros((heads, HD), jnp.float32)
    rows = lax.dynamic_update_slice(rows, gain, (lax.axis_index("head") * gain.shape[0], 0))
    parts = []
    for _ in range(3):
        part = lax.reduce_precision(rows, 8, 7)
        parts.append(packed(part))
        rows = rows - part
    parts.append(jnp.zeros((-3 * heads % HD, HD), jnp.bfloat16))
    return jnp.concatenate(parts).reshape(-1, HD, HD)


def per_device(queries, key_vectors, value_vectors, out_gain):
    heads = queries.shape[1] // HD
    side = (lax.axis_index("head") % 2).astype(jnp.int32).reshape(1)
    gain_parts = parts_of(out_gain, heads)


    firsts, sizes, scans, locals_by_piece = [], [], [], {}
    first = 0
    for size, count in SIZES:
        own, other = states_of(side, key_vectors, value_vectors, first, size, count)
        for piece in range(count):
            part = slice(piece * size // 2, (piece + 1) * size // 2)
            scans.append(scan_of(own[part], other[part], None if scans else gain_parts))
            firsts.append(first)
            sizes.append(size)
            first += size
            next(scans[-1])

    count = len(scans)
    done, out, gain = [[] for _ in scans], None, None
    for step in STEPS.split():
        piece, *wait_for = step.split(",")
        piece = int(piece)
        wait_for = [done[int(item[0])][int(item[1])] for item in wait_for]
        swap = len(done[piece])
        if swap == LOCAL_SWAP:
            local = locals_of(queries, key_vectors, value_vectors, firsts[piece], sizes[piece])
            wait_for += [local] if LOCAL_TIE else []
        result = scans[piece].send(wait_for)
        if swap == LOCAL_SWAP:
            locals_by_piece[piece] = local
        if isinstance(result, tuple):
            mine, theirs, extra = result
            if extra is not None:
                rows = extra.reshape(-1, HD)
                gain = rows[:heads] + rows[heads : 2 * heads] + rows[2 * heads : 3 * heads]
                gain = gain.reshape(heads, 1, HD)
            out = outputs_of(side, queries, locals_by_piece[piece], mine, theirs, gain, firsts[piece], out)
            result = out
        done[piece].append(result)
    return out


def solution(mesh):
    return jax.shard_map(
        per_device,
        mesh=mesh,
        in_specs=(
            P(("seq", "head"), None),
            P(("seq", "head"), None),
            P(("seq", "head"), None),
            P("head", None),
        ),
        out_specs=P(("seq", "head"), None),
        check_vma=False,
    )
```

```python
import functools

import jax
import jax.numpy as jnp
from jax import lax
from jax.experimental import pallas as pl
from jax.experimental.pallas import tpu as pltpu
from jax.sharding import PartitionSpec as P

HD = 128
SIZES = ((16, 1),) * 4
LOCAL_STEP = 8
LOCAL_AFTER = (-1, 1)
KEEP = False
LOCAL_SWAP = 4
LOCAL_TIE = True
STEPS = ((0,), (1, (0, 0)), (2, (1, 0)), (3, (2, 0)), (0,), (1,), (2,), (3,), (0,), (1,), (2,), (3,), (0,), (1,), (2,), (3,), (0,), (1,), (2,), (3,), (0,), (1,), (2,), (3,), (0,), (1,), (2,), (3,))
VMEM = 24 << 20


def f32(block):
    return block.astype(jnp.float32)


def packed(total):
    return total.astype(jnp.bfloat16)


def added(*terms):
    return functools.reduce(jnp.add, [f32(term) for term in terms])


def kept(condition, block):
    return jnp.where(condition, f32(block), 0.0)


def state_kernel(side_ref, key_ref, value_ref, mine_ref, theirs_ref):
    half = mine_ref.shape[0]
    for side, state_ref in enumerate((mine_ref, theirs_ref)):
        base = (side_ref[0] ^ side) * half
        for head in range(half):
            columns = pl.ds(pl.multiple_of((base + head) * HD, HD), HD)
            state = lax.dot_general(
                key_ref[:, columns],
                value_ref[:, columns],
                (((0,), (0,)), ((), ())),
                preferred_element_type=jnp.float32,
            )
            state_ref[head] = packed(state)


def states_of(side, key_vectors, value_vectors, first, step, steps):
    tokens, half = key_vectors.shape[0], step // 2
    tokens_spec = pl.BlockSpec((tokens, step * HD), lambda i, side: (0, first // step + i))
    side_spec = pl.BlockSpec((half, HD, HD), lambda i, side: (i, 0, 0))
    half_shape = jax.ShapeDtypeStruct((steps * half, HD, HD), jnp.bfloat16)
    return pl.pallas_call(
        state_kernel,
        grid_spec=pltpu.PrefetchScalarGridSpec(
            num_scalar_prefetch=1,
            grid=(steps,),
            in_specs=[tokens_spec, tokens_spec],
            out_specs=[side_spec, side_spec],
        ),
        out_shape=[half_shape, half_shape],
        compiler_params=pltpu.CompilerParams(vmem_limit_bytes=VMEM),
        cost_estimate=pl.CostEstimate(
            flops=2 * tokens * HD * HD * step * steps,
            bytes_accessed=2 * step * steps * HD * (2 * tokens + HD),
            transcendentals=0,
        ),
    )(side, key_vectors, value_vectors)


def local_kernel(query_ref, key_ref, value_ref, *refs):
    local_ref = refs[-1]
    tokens = query_ref.shape[0]
    rows = lax.broadcasted_iota(jnp.int32, (tokens, tokens), 0)
    causal = rows >= lax.broadcasted_iota(jnp.int32, (tokens, tokens), 1)
    for head in range(query_ref.shape[1] // HD):
        columns = slice(head * HD, (head + 1) * HD)
        scores = lax.dot_general(
            query_ref[:, columns],
            key_ref[:, columns],
            (((1,), (1,)), ((), ())),
            preferred_element_type=jnp.float32,
        )
        scores = packed(jnp.where(causal, scores, 0.0))
        local_ref[:, columns] = jnp.dot(scores, value_ref[:, columns], preferred_element_type=jnp.float32)


def locals_of(queries, key_vectors, value_vectors, first, count, wait_for):
    tokens, step = queries.shape[0], min(count, LOCAL_STEP)
    tokens_spec = pl.BlockSpec((tokens, step * HD), lambda i: (0, first // step + i))
    return pl.pallas_call(
        local_kernel,
        grid=(count // step,),
        in_specs=[tokens_spec] * 3 + [pl.BlockSpec(memory_space=pl.ANY)] * len(wait_for),
        out_specs=pl.BlockSpec((tokens, step * HD), lambda i: (0, i)),
        out_shape=jax.ShapeDtypeStruct((tokens, count * HD), jnp.float32),
        compiler_params=pltpu.CompilerParams(vmem_limit_bytes=VMEM),
        cost_estimate=pl.CostEstimate(
            flops=4 * tokens * HD * count * tokens,
            bytes_accessed=count * HD * 10 * tokens,
            transcendentals=0,
        ),
    )(queries, key_vectors, value_vectors, *wait_for)


def output_kernel(side_ref, query_ref, local_ref, mine_ref, theirs_ref, gain_ref, *refs):
    out_ref = refs[-1]
    own = pl.program_id(0) == 0
    for head in range(mine_ref.shape[0]):
        columns = slice(head * HD, (head + 1) * HD)
        carried = jnp.where(own, mine_ref[head], theirs_ref[head])
        raw = jnp.dot(query_ref[:, columns], carried, preferred_element_type=jnp.float32) + local_ref[:, columns]
        scale = lax.rsqrt(jnp.mean(raw * raw, axis=-1, keepdims=True) + 1e-06)
        out_ref[:, columns] = packed(raw * scale * gain_ref[head])


def outputs_of(side, queries, local, mine, theirs, gain, first, before):
    tokens, half = queries.shape[0], mine.shape[0]
    tokens_spec = pl.BlockSpec((tokens, half * HD), lambda i, side: (0, first // half + (side[0] ^ i)))
    local_spec = pl.BlockSpec((tokens, half * HD), lambda i, side: (0, side[0] ^ i))
    side_spec = pl.BlockSpec((half, HD, HD), lambda i, side: (0, 0, 0))
    gain_spec = pl.BlockSpec((half, 1, HD), lambda i, side: (first // half + (side[0] ^ i), 0, 0))
    operands = [queries, local, mine, theirs, gain]
    in_specs = [tokens_spec, local_spec, side_spec, side_spec, gain_spec]
    aliases = {}
    if before is not None:
        operands.append(before)
        in_specs.append(pl.BlockSpec(memory_space=pl.ANY))
        aliases = {6: 0}
    return pl.pallas_call(
        output_kernel,
        grid_spec=pltpu.PrefetchScalarGridSpec(
            num_scalar_prefetch=1, grid=(2,), in_specs=in_specs, out_specs=tokens_spec
        ),
        out_shape=jax.ShapeDtypeStruct(queries.shape, jnp.bfloat16),
        input_output_aliases=aliases,
        compiler_params=pltpu.CompilerParams(vmem_limit_bytes=VMEM),
        cost_estimate=pl.CostEstimate(
            flops=4 * tokens * HD * half * HD,
            bytes_accessed=2 * half * HD * (8 * tokens + HD),
            transcendentals=2 * tokens * half,
        ),
    )(side, *operands)


def after(block, done):
    return lax.optimization_barrier((block, *done))[0] if done else block


def kept_whole(total):
    return lax.optimization_barrier(total) if KEEP else total


def swapped(block, axis, step):
    return lax.ppermute(block, axis, [(i, i ^ step) for i in range(lax.axis_size(axis))])


def scan_of(mine, theirs, extra):
    half, side = mine.shape[0], lax.axis_index("head") % 2
    done = yield
    sent = theirs if extra is None else jnp.concatenate([theirs, extra])
    arrived = swapped(after(sent, done), "head", 1)
    done = yield arrived
    neighbour = arrived[:half]
    whole = kept_whole(added(mine, neighbour))
    if extra is not None:
        extra = added(extra, arrived[half:])
    pieces = []
    for axis, step in [("head", 2), ("seq", 1)]:
        index = lax.axis_index(axis)
        while step < lax.axis_size(axis):
            sent = packed(whole)
            if extra is not None and axis == "head":
                sent = jnp.concatenate([sent, packed(extra)])
            arrived = swapped(after(sent, done), axis, step)
            done = ()
            if (axis, step) in (("head", 2), ("seq", 1), ("seq", 2), ("seq", 4)):
                done = yield arrived
                if (axis, step) != ("head", 2):
                    arrived, done = after(arrived, done), ()
            pieces.append(kept(index & step != 0, arrived[:half]))
            whole = kept_whole(whole + f32(arrived[:half]))
            if extra is not None and axis == "head":
                extra = extra + f32(arrived[half:])
            step *= 2
    earlier = functools.reduce(jnp.add, pieces)
    carried_mine = packed(earlier + kept(side == 1, neighbour))
    carried_theirs = packed(earlier + kept(side == 0, mine))
    arrived = swapped(after(carried_theirs, done), "head", 1)
    arrived = after(arrived, (yield arrived))
    yield carried_mine, arrived, extra


def parts_of(gain, heads):
    rows = jnp.zeros((heads, HD), jnp.float32)
    rows = lax.dynamic_update_slice(rows, gain, (lax.axis_index("head") * gain.shape[0], 0))
    parts = []
    for _ in range(3):
        part = lax.reduce_precision(rows, 8, 7)
        parts.append(packed(part))
        rows = rows - part
    parts.append(jnp.zeros((-3 * heads % HD, HD), jnp.bfloat16))
    return jnp.concatenate(parts).reshape(-1, HD, HD)


def per_device(queries, key_vectors, value_vectors, out_gain):
    heads = queries.shape[1] // HD
    side = (lax.axis_index("head") % 2).astype(jnp.int32).reshape(1)
    gain_parts = parts_of(out_gain, heads)


    firsts, sizes, scans, locals_by_piece = [], [], [], {}
    first = 0
    for size, count in SIZES:
        own, other = states_of(side, key_vectors, value_vectors, first, size, count)
        for piece in range(count):
            part = slice(piece * size // 2, (piece + 1) * size // 2)
            scans.append(scan_of(own[part], other[part], None if scans else gain_parts))
            firsts.append(first)
            sizes.append(size)
            first += size
            next(scans[-1])

    count = len(scans)
    done, out, gain = [[] for _ in scans], None, None
    for piece, *wait_for in STEPS:
        wait_for = [done[other][swap] for other, swap in wait_for]
        swap = len(done[piece])
        if swap == LOCAL_SWAP:
            other, brought = piece + LOCAL_AFTER[0], LOCAL_AFTER[1]
            before = [done[other][brought]] if 0 <= other and len(done[other]) > brought else []
            local = locals_of(queries, key_vectors, value_vectors, firsts[piece], sizes[piece], before)
            wait_for += [local] if LOCAL_TIE else []
        result = scans[piece].send(wait_for)
        if swap == LOCAL_SWAP:
            locals_by_piece[piece] = local
        if isinstance(result, tuple):
            mine, theirs, extra = result
            if extra is not None:
                rows = extra.reshape(-1, HD)
                gain = rows[:heads] + rows[heads : 2 * heads] + rows[2 * heads : 3 * heads]
                gain = gain.reshape(heads, 1, HD)
            out = outputs_of(side, queries, locals_by_piece[piece], mine, theirs, gain, firsts[piece], out)
            result = out
        done[piece].append(result)
    return out


def solution(mesh):
    return jax.shard_map(
        per_device,
        mesh=mesh,
        in_specs=(
            P(("seq", "head"), None),
            P(("seq", "head"), None),
            P(("seq", "head"), None),
            P("head", None),
        ),
        out_specs=P(("seq", "head"), None),
        check_vma=False,
    )
```

```python
import functools

import jax
import jax.numpy as jnp
from jax import lax
from jax.experimental import pallas as pl
from jax.experimental.pallas import tpu as pltpu
from jax.sharding import PartitionSpec as P

HD = 128
SIZES = ((0, 16, 1), (16, 16, 3))
OUT_ORDER = (0, 1, 3, 2)
GAIN_PIECE = 0
SEQ_FIRST = (False, False, False, True)
SHARED = False
LOCAL_STEP = 8
LOCAL_AFTER = ((0, 0), (0, 1), (1, 1), (1, 1))
LOCAL_SWAP = (4, 4, 4, 5)
LOCAL_TIE = True
STEPS = ((0,), (3, (0, 0)), (1, (3, 0)), (2, (1, 0)), (0,), (1,), (2,), (3,), (0,), (1,), (2,), (3,), (0,), (1,), (2,), (3,), (0,), (1,), (2,), (3, (2, 2)), (0,), (1,), (2,), (3,), (0,), (1,), (2,), (3,))
VMEM = 24 << 20


def f32(block):
    return block.astype(jnp.float32)


def packed(total):
    return total.astype(jnp.bfloat16)


def added(*terms):
    return functools.reduce(jnp.add, [f32(term) for term in terms])


def kept(condition, block):
    return jnp.where(condition, f32(block), 0.0)


def state_kernel(side_ref, key_ref, value_ref, *refs, first):
    *state_refs, keys, values, sems = refs
    half = state_refs[0].shape[0]
    copies = []
    for part in range(len(state_refs)):
        own = side_ref[0] if part % 2 else 1 - side_ref[0]
        columns = pl.ds(pl.multiple_of((first + (part // 2 * 2 + own) * half) * HD, HD), half * HD)
        for which, (ref, buffer) in enumerate(((key_ref, keys), (value_ref, values))):
            copies.append(pltpu.make_async_copy(ref.at[:, columns], buffer.at[part], sems.at[part, which]))
            copies[-1].start()
    for part, state_ref in enumerate(state_refs):
        copies[2 * part].wait()
        copies[2 * part + 1].wait()
        for head in range(half):
            columns = slice(head * HD, (head + 1) * HD)
            state = lax.dot_general(
                keys[part, :, columns],
                values[part, :, columns],
                (((0,), (0,)), ((), ())),
                preferred_element_type=jnp.float32,
            )
            state_ref[head] = packed(state)


def states_of(side, key_vectors, value_vectors, first, size, count):
    tokens, half = key_vectors.shape[0], size // 2
    parts = 2 * count
    buffer = pltpu.VMEM((parts, tokens, half * HD), jnp.bfloat16)
    return pl.pallas_call(
        functools.partial(state_kernel, first=first),
        grid_spec=pltpu.PrefetchScalarGridSpec(
            num_scalar_prefetch=1,
            grid=(1,),
            in_specs=[pl.BlockSpec(memory_space=pl.ANY)] * 2,
            out_specs=[pl.BlockSpec((half, HD, HD), lambda i, side: (0, 0, 0))] * parts,
            scratch_shapes=[buffer, buffer, pltpu.SemaphoreType.DMA((parts, 2))],
        ),
        out_shape=[jax.ShapeDtypeStruct((half, HD, HD), jnp.bfloat16)] * parts,
        compiler_params=pltpu.CompilerParams(vmem_limit_bytes=VMEM),
        cost_estimate=pl.CostEstimate(
            flops=2 * tokens * HD * HD * size * count,
            bytes_accessed=2 * size * count * HD * (2 * tokens + HD),
            transcendentals=0,
        ),
    )(side, key_vectors, value_vectors)


def local_kernel(query_ref, key_ref, value_ref, *refs):
    local_ref = refs[-1]
    tokens = query_ref.shape[0]
    rows = lax.broadcasted_iota(jnp.int32, (tokens, tokens), 0)
    causal = rows >= lax.broadcasted_iota(jnp.int32, (tokens, tokens), 1)
    for head in range(query_ref.shape[1] // HD):
        columns = slice(head * HD, (head + 1) * HD)
        scores = lax.dot_general(
            query_ref[:, columns],
            key_ref[:, columns],
            (((1,), (1,)), ((), ())),
            preferred_element_type=jnp.float32,
        )
        scores = packed(jnp.where(causal, scores, 0.0))
        local_ref[:, columns] = jnp.dot(scores, value_ref[:, columns], preferred_element_type=jnp.float32)


def locals_of(queries, key_vectors, value_vectors, first, count, wait_for):
    tokens, step = queries.shape[0], min(count, LOCAL_STEP)
    tokens_spec = pl.BlockSpec((tokens, step * HD), lambda i: (0, first // step + i))
    return pl.pallas_call(
        local_kernel,
        grid=(count // step,),
        in_specs=[tokens_spec] * 3 + [pl.BlockSpec(memory_space=pl.ANY)] * len(wait_for),
        out_specs=pl.BlockSpec((tokens, step * HD), lambda i: (0, i)),
        out_shape=jax.ShapeDtypeStruct((tokens, count * HD), jnp.float32),
        compiler_params=pltpu.CompilerParams(vmem_limit_bytes=VMEM),
        cost_estimate=pl.CostEstimate(
            flops=4 * tokens * HD * count * tokens,
            bytes_accessed=count * HD * 10 * tokens,
            transcendentals=0,
        ),
    )(queries, key_vectors, value_vectors, *wait_for)


def output_kernel(side_ref, query_ref, local_ref, mine_ref, theirs_ref, gain_ref, *refs):
    out_ref = refs[-1]
    own = pl.program_id(0) == 0
    for head in range(mine_ref.shape[0]):
        columns = slice(head * HD, (head + 1) * HD)
        carried = jnp.where(own, mine_ref[head], theirs_ref[head])
        raw = jnp.dot(query_ref[:, columns], carried, preferred_element_type=jnp.float32) + local_ref[:, columns]
        scale = lax.rsqrt(jnp.mean(raw * raw, axis=-1, keepdims=True) + 1e-06)
        out_ref[:, columns] = packed(raw * scale * gain_ref[head])


def outputs_of(side, queries, local, mine, theirs, gain, first, before):
    tokens, half = queries.shape[0], mine.shape[0]
    tokens_spec = pl.BlockSpec((tokens, half * HD), lambda i, side: (0, first // half + (side[0] ^ i)))
    local_spec = pl.BlockSpec((tokens, half * HD), lambda i, side: (0, side[0] ^ i))
    side_spec = pl.BlockSpec((half, HD, HD), lambda i, side: (0, 0, 0))
    gain_spec = pl.BlockSpec((half, 1, HD), lambda i, side: (first // half + (side[0] ^ i), 0, 0))
    operands = [queries, local, mine, theirs, gain]
    in_specs = [tokens_spec, local_spec, side_spec, side_spec, gain_spec]
    aliases = {}
    if before is not None:
        operands.append(before)
        in_specs.append(pl.BlockSpec(memory_space=pl.ANY))
        aliases = {6: 0}
    return pl.pallas_call(
        output_kernel,
        grid_spec=pltpu.PrefetchScalarGridSpec(
            num_scalar_prefetch=1, grid=(2,), in_specs=in_specs, out_specs=tokens_spec
        ),
        out_shape=jax.ShapeDtypeStruct(queries.shape, jnp.bfloat16),
        input_output_aliases=aliases,
        compiler_params=pltpu.CompilerParams(vmem_limit_bytes=VMEM),
        cost_estimate=pl.CostEstimate(
            flops=4 * tokens * HD * half * HD,
            bytes_accessed=2 * half * HD * (8 * tokens + HD),
            transcendentals=2 * tokens * half,
        ),
    )(side, *operands)


def after(block, done):
    return lax.optimization_barrier((block, *done))[0] if done else block


def swapped(block, axis, step):
    return lax.ppermute(block, axis, [(i, i ^ step) for i in range(lax.axis_size(axis))])


def scan_of(mine, theirs, extra, seq_first):
    half, place, index = mine.shape[0], lax.axis_index("head"), lax.axis_index("seq")
    side, core = place % 2, index % 2
    done = yield
    sent = theirs if extra is None else jnp.concatenate([theirs, extra])
    arrived = swapped(after(sent, done), "head", 1)
    done = yield arrived
    neighbour = arrived[:half]
    pair = added(mine, neighbour)
    if extra is not None:
        extra = added(extra, arrived[half:])

    whole, terms = pair, []
    step = 2
    while step < lax.axis_size("head") and not seq_first:
        sent = packed(whole)
        if extra is not None:
            sent = jnp.concatenate([sent, packed(extra)])
        arrived = swapped(after(sent, done), "head", step)
        done = ()
        if step == 2:
            done = yield arrived
        terms.append(kept(place & step != 0, arrived[:half]))
        whole = whole + f32(arrived[:half])
        if extra is not None:
            extra = extra + f32(arrived[half:])
        step *= 2

    arrived = swapped(after(packed(whole), done), "seq", 1)
    arrived = after(arrived, (yield arrived))
    terms.append(kept(core == 1, arrived))
    whole = whole + f32(arrived)
    if SHARED:
        part = half // 2
        whole = jnp.where(core == 0, whole[:part], whole[part:])
    chips, step = [], 2
    while step < lax.axis_size("seq"):
        arrived = swapped(packed(whole), "seq", step)
        if step <= 4:
            arrived = after(arrived, (yield arrived))
        chips.append(kept(index & step != 0, arrived))
        whole = whole + f32(arrived)
        step *= 2
    if SHARED:
        chips = packed(functools.reduce(jnp.add, chips))
        other = swapped(chips, "seq", 1)
        chips = [f32(jnp.concatenate([jnp.where(core == 0, chips, other), jnp.where(core == 0, other, chips)]))]
    earlier = functools.reduce(jnp.add, terms + chips)

    if seq_first:
        sent = packed(earlier + jnp.where(place & 2 == 0, pair, 0.0))
        arrived = swapped(sent, "head", 2)
        done = yield arrived
        earlier = earlier + f32(arrived)
    else:
        done = ()
    carried_mine = packed(earlier + kept(side == 1, neighbour))
    carried_theirs = packed(earlier + kept(side == 0, mine))
    arrived = swapped(after(carried_theirs, done), "head", 1)
    arrived = after(arrived, (yield arrived))
    yield carried_mine, arrived, extra


def parts_of(gain, heads):
    rows = jnp.zeros((heads, HD), jnp.float32)
    rows = lax.dynamic_update_slice(rows, gain, (lax.axis_index("head") * gain.shape[0], 0))
    parts = []
    for _ in range(3):
        part = lax.reduce_precision(rows, 8, 7)
        parts.append(packed(part))
        rows = rows - part
    parts.append(jnp.zeros((-3 * heads % HD, HD), jnp.bfloat16))
    return jnp.concatenate(parts).reshape(-1, HD, HD)


def per_device(queries, key_vectors, value_vectors, out_gain):
    heads = queries.shape[1] // HD
    side = (lax.axis_index("head") % 2).astype(jnp.int32).reshape(1)
    gain_parts = parts_of(out_gain, heads)


    firsts, sizes, scans, locals_by_piece = [], [], [], {}
    for first, size, count in SIZES:
        states = states_of(side, key_vectors, value_vectors, first, size, count)
        for number, (theirs, mine) in enumerate(zip(states[0::2], states[1::2])):
            seq_first = SEQ_FIRST[len(scans)] and lax.axis_size("head") == 4
            scans.append(scan_of(mine, theirs, gain_parts if len(scans) == GAIN_PIECE else None, seq_first))
            firsts.append(first + number * size)
            sizes.append(size)
            next(scans[-1])

    count = len(scans)
    done, out = [[] for _ in scans], None
    for piece, *wait_for in STEPS:
        wait_for = [done[other][swap] for other, swap in wait_for]
        swap = len(done[piece])
        if swap == LOCAL_SWAP[piece]:
            other, brought = LOCAL_AFTER[piece]
            before = [done[other][brought]] if len(done[other]) > brought else []
            local = locals_of(queries, key_vectors, value_vectors, firsts[piece], sizes[piece], before)
            wait_for += [local] if LOCAL_TIE else []
        result = scans[piece].send(wait_for)
        if swap == LOCAL_SWAP[piece]:
            locals_by_piece[piece] = local
        done[piece].append(result)
    rows = done[GAIN_PIECE][-1][2].reshape(-1, HD)
    gain = (rows[:heads] + rows[heads : 2 * heads] + rows[2 * heads : 3 * heads]).reshape(heads, 1, HD)
    for piece in OUT_ORDER:
        mine, theirs, _ = done[piece][-1]
        out = outputs_of(side, queries, locals_by_piece[piece], mine, theirs, gain, firsts[piece], out)
    return out


def solution(mesh):
    return jax.shard_map(
        per_device,
        mesh=mesh,
        in_specs=(
            P(("seq", "head"), None),
            P(("seq", "head"), None),
            P(("seq", "head"), None),
            P("head", None),
        ),
        out_specs=P(("seq", "head"), None),
        check_vma=False,
    )
```
